768 devices in a mesh: grp: 96 (over y, z), sub: 8 (over x, core).
Axes of the slice: x: 4, y: 8, z: 12, core: 2. Of those that a mesh axis runs over, the one named last changes fastest.
Arguments:
- multipoles: bfloat16 [786432, 128], P(('grp', 'sub')), may hold values from -6 to 6
- up_ops: bfloat16 [8, 128, 128], replicated, may hold values from -0.1875 to 0.1875
- down_ops: bfloat16 [8, 128, 128], replicated, may hold values from -0.5 to 0.5
- far_ops: bfloat16 [189, 128, 128], replicated, may hold values from -0.0390625 to 0.0390625
- sources5: int32 [189, 98304], P(None, ('grp', 'sub')), may hold values from -1 to 1407, as said below
- sources4: int32 [189, 12288], P(None, ('grp', 'sub')), may hold values from -1 to 127, as said below
- sources3: int32 [189, 1536], P(None, ('grp', 'sub')), may hold values from -1 to 1535, as said below
- send_boxes: int32 [768, 96, 4], P(('grp', 'sub')), may hold values from 0 to 127
- send_counts: int32 [768, 96], P(('grp', 'sub')), may hold values from 0 to 4, as said below
Outputs:
- local_six: float32 [786432, 128], P(('grp', 'sub'))
The draws below stay inside these ranges and needn't reach their ends.
Inputs may be any that keep to these rules, and one draw needn't show every extreme that they name: `sources5`: -1 means no source of that class; smaller than 1024 names a block of the target group's level-5 boxes, otherwise the entry minus that is j * 4 + k, a slot received from grp index j. `sources4`: -1 means no source; otherwise a block of the target group's level-4 boxes. `sources3`: -1 means no source; otherwise a level-3 box. `send_counts`: in every draw one grp index receives 4 filled slots from every device.
All inputs are finite; a program needn't handle non-finite values.
Results may differ from the reference program's by a relative error of at most 0.012.
Values may be sent and summed in bfloat16 or wider, within the bound.
A program may use at most 64 MiB of HBM per device.

```python
import jax
import jax.numpy as jnp
from jax import lax

K = 128
CLASSES = 189
CAP = 4
BOX_DEV = 1024
BOXES6 = 786432
BOXES5 = 98304
BOXES4 = 12288
BOXES3 = 1536
N_GRP = 96
N_SUB = 8
DEVICES = 768


def draw_sources5(key, part):
    key = jax.random.fold_in(key, 11)
    key_kind, key_near, key_far = jax.random.split(key, 3)
    shape = (CLASSES, BOXES5)
    span = N_SUB * (BOX_DEV // 8)
    kind = jax.random.randint(key_kind, shape, 0, 10)
    near = jax.random.randint(key_near, shape, 0, span)
    remote = span + jax.random.randint(key_far, shape, 0, N_GRP * CAP)
    return jnp.where(kind == 0, -1, jnp.where(kind < 5, near, remote)).astype(jnp.int32)


def draw_sources4(key, part):
    key = jax.random.fold_in(key, 12)
    key_kind, key_near = jax.random.split(key, 2)
    shape = (CLASSES, BOXES4)
    kind = jax.random.randint(key_kind, shape, 0, 10)
    near = jax.random.randint(key_near, shape, 0, N_SUB * (BOX_DEV // 64))
    return jnp.where(kind == 0, -1, near).astype(jnp.int32)


def draw_sources3(key, part):
    key = jax.random.fold_in(key, 13)
    key_kind, key_near = jax.random.split(key, 2)
    shape = (CLASSES, BOXES3)
    kind = jax.random.randint(key_kind, shape, 0, 10)
    near = jax.random.randint(key_near, shape, 0, BOXES3)
    return jnp.where(kind == 0, -1, near).astype(jnp.int32)


def draw_send_counts(key, part):
    key = jax.random.fold_in(key, 14)
    key_base, key_busy = jax.random.split(key, 2)
    base = jax.random.randint(key_base, (DEVICES, N_GRP), 0, CAP + 1)
    busiest = jax.random.randint(key_busy, (), 0, N_GRP)
    columns = jnp.arange(N_GRP, dtype=jnp.int32)[None, :]
    return jnp.where(columns == busiest, CAP, base).astype(jnp.int32)


def set_ends(array, rng, low, top_value):
    place = [jax.random.randint(jax.random.fold_in(rng, axis), (), 0, length) for axis, length in enumerate(array.shape)]
    longest = array.shape.index(max(array.shape))
    beside = place[:longest] + [(place[longest] + 1) % array.shape[longest]] + place[longest + 1:]
    return array.at[tuple(place)].set(low).at[tuple(beside)].set(top_value)


def steps_of(stream_key, shape, cuts, least, high):
    loudness, own = 1.0, jax.random.fold_in(stream_key, 6)
    for dim, shards_of in cuts:
        draws = jnp.exp(jax.random.uniform(jax.random.fold_in(own, dim), (shards_of,), jnp.float32, least / len(cuts), high / len(cuts)))
        loudness = loudness * jnp.repeat(draws, shape[dim] // shards_of).reshape([-1 if axis == dim else 1 for axis in range(len(shape))])
    return loudness


def centred(stream_key, dims, deviation, bound, cuts=(), held_as=jnp.bfloat16):
    values = jax.random.normal(stream_key, dims, jnp.float32) * deviation
    if len(cuts) > 0:
        values = steps_of(stream_key, dims, cuts, -0.22, 0.18) * values
    return jnp.clip(values, min=-bound, max=bound).astype(held_as)


def setup_inputs(seed: int = 0) -> dict:
    seeds = jax.random.split(jax.random.key(seed), 10)
    multipoles = centred(seeds[0], (BOXES6, K), 1.0, 6.0, ((0, 768),))
    up_ops = centred(seeds[1], (8, K, K), (8 * K) ** -0.5, 0.1875)
    down_ops = centred(seeds[2], (8, K, K), K ** -0.5, 0.5)
    far_ops = centred(seeds[3], (CLASSES, K, K), (K * CLASSES) ** -0.5, 0.0390625)
    sources5 = draw_sources5(jax.random.fold_in(seeds[9], 71), 0)
    sources4 = draw_sources4(jax.random.fold_in(seeds[9], 71), 0)
    sources3 = draw_sources3(jax.random.fold_in(seeds[9], 71), 0)
    send_boxes = set_ends(jax.random.randint(seeds[7], (DEVICES, N_GRP, CAP), 0, BOX_DEV // 8), jax.random.fold_in(seeds[7], 1), 0, (BOX_DEV // 8) - 1).astype(jnp.int32)
    send_counts = draw_send_counts(jax.random.fold_in(seeds[9], 71), 0)
    return dict(multipoles=multipoles, up_ops=up_ops, down_ops=down_ops, far_ops=far_ops, sources5=sources5, sources4=sources4, sources3=sources3, send_boxes=send_boxes, send_counts=send_counts)


def ascend(children, up_ops):
    coeffs = children.shape[1]
    stacked = children.reshape(children.shape[0] // 8, 8 * coeffs)
    return jnp.dot(stacked, up_ops.reshape(8 * coeffs, coeffs), preferred_element_type=jnp.float32).astype(jnp.bfloat16)


def descend(parent, down_ops):
    coeffs = parent.shape[1]
    spread = jnp.transpose(down_ops, (1, 0, 2)).reshape(coeffs, 8 * coeffs)
    return jnp.dot(parent, spread, preferred_element_type=jnp.float32).reshape(parent.shape[0] * 8, coeffs)


def far_scan(source_rows, sources, far_ops):
    def accumulate(running, entries):
        lookup, operator = entries
        picked = source_rows[jnp.maximum(lookup, 0)]
        picked = jnp.where((lookup >= 0)[:, None], picked, jnp.zeros_like(picked))
        return running + jnp.dot(picked, operator, preferred_element_type=jnp.float32), None
    start = jnp.zeros((sources.shape[1], source_rows.shape[1]), jnp.float32)
    running, unused = lax.scan(accumulate, start, (sources, far_ops))
    return running


def reference(multipoles, up_ops, down_ops, far_ops, sources5, sources4, sources3, send_boxes, send_counts):
    poles_five = ascend(multipoles, up_ops)
    poles_four = ascend(poles_five, up_ops)
    poles_three = ascend(poles_four, up_ops)
    local_three = far_scan(poles_three, sources3, far_ops).astype(jnp.bfloat16)
    block_four = BOX_DEV // 64
    block_five = BOX_DEV // 8
    group_four = jnp.arange(BOXES4, dtype=jnp.int32) // (block_four * N_SUB)
    global_four = jnp.where(sources4 >= 0, sources4 + (group_four * (block_four * N_SUB))[None, :], -1)
    local_four = (descend(local_three, down_ops) + far_scan(poles_four, global_four, far_ops)).astype(jnp.bfloat16)
    devices = jnp.arange(DEVICES, dtype=jnp.int32)
    group_of = devices // N_SUB
    column = devices % N_SUB
    peer_ids = jnp.arange(N_GRP, dtype=jnp.int32)
    sender = peer_ids[None, :] * N_SUB + column[:, None]
    chosen = send_boxes[sender, group_of[:, None]]
    sent_count = send_counts[sender, group_of[:, None]]
    filled = jnp.arange(CAP, dtype=jnp.int32)[None, None, :] < sent_count[:, :, None]
    store_ids = jnp.where(filled, sender[:, :, None] * block_five + chosen, BOXES5).astype(jnp.int32)
    flattened = store_ids.reshape(DEVICES * N_GRP * CAP)
    source_rows = jnp.concatenate([poles_five, jnp.zeros((1, poles_five.shape[1]), poles_five.dtype)], 0)
    span = N_SUB * block_five
    target_dev = jnp.arange(BOXES5, dtype=jnp.int32) // block_five
    remote = jnp.maximum(sources5 - span, 0) + (target_dev * (N_GRP * CAP))[None, :]
    inside = sources5 + ((target_dev // N_SUB) * span)[None, :]
    global_five = jnp.where(sources5 < 0, -1, jnp.where(sources5 < span, inside, flattened[remote]))
    local_five = (descend(local_four, down_ops) + far_scan(source_rows, global_five, far_ops)).astype(jnp.bfloat16)
    return descend(local_five, down_ops)
```

```python
import functools

import jax
import jax.numpy as jnp
from jax import lax
from jax.experimental import pallas as pl
from jax.experimental.pallas import tpu as pltpu
from jax.sharding import PartitionSpec as P

K = 128
CLASSES = 189
CAP = 4
GROUPS = 96
SUBS = 8
SECT = GROUPS // SUBS
NEAR = 1024
EMPTY = 1535
STEP = 9
STEPS = CLASSES // STEP
MESH = pl.DeviceIdType.MESH
F32 = jnp.float32
BF16 = jnp.bfloat16


def mm(a, b):
    return jnp.dot(a, b, preferred_element_type=F32)


def ascend(rows, count, wide, up):
    wide[pl.ds(0, 8 * count), :] = rows.astype(F32)
    total = jnp.zeros((count, K), F32)
    for c in range(8):
        total += mm(wide[pl.ds(c, count, stride=8), :].astype(BF16), up[c])
    return total.astype(BF16)


def column(block, c):
    return jnp.take_along_axis(block, jnp.full(block.shape, c, jnp.int32), axis=1)


def kernel(
    mult, up, down, src5, src4, src3, boxes, counts, ops_hbm, out,
    five, pack32, pack, slots, store, tops, ops, hot5, hot3, idx5, idx4, idx3, tmp, wide, picks3,
    ops_sem, five_send, five_recv, slot_send, slot_recv, top_send, top_recv, rest_send, rest_recv,
):
    g = lax.axis_index("grp")
    s = lax.axis_index("sub")
    gs = lax.rem(g, SUBS)
    twin = gs == s

    fetch = pltpu.make_async_copy(ops_hbm, ops, ops_sem)
    fetch.start()

    barrier = pltpu.get_barrier_semaphore()

    def greet(i, carry):
        pl.semaphore_signal(barrier, inc=1, device_id=(lax.rem(g + i, GROUPS), s), device_id_type=MESH)
        return carry

    for i in range(1, SUBS):
        pl.semaphore_signal(barrier, inc=1, device_id=(g, lax.rem(s + i, SUBS)), device_id_type=MESH)
    lax.fori_loop(1, GROUPS, greet, 0)

    def partner(m):
        j = s + SUBS * m
        return j, jnp.logical_not(jnp.logical_and(twin, j == g))

    def greet_tops(m, carry):
        j, other = partner(m)

        @pl.when(other)
        def _():
            pl.semaphore_signal(barrier, inc=1, device_id=(j, gs), device_id_type=MESH)

        return carry

    lax.fori_loop(0, SECT, greet_tops, 0)

    mine = ascend(mult[...], 128, wide, up)
    own = pl.multiple_of(s * 128, 128)
    five[pl.ds(own, 128), :] = mine

    box = lax.broadcasted_iota(jnp.int32, (128, GROUPS), 0)
    for k in range(CAP):
        hit = jnp.logical_and(box == boxes[k : k + 1, :], counts[...] > k)
        chosen = lax.dot_general(
            jnp.where(hit, 1.0, 0.0).astype(BF16), mine, (((0,), (0,)), ((), ())), preferred_element_type=F32
        )
        pack32[pl.ds(k, GROUPS, stride=CAP), :] = chosen
    pack[...] = pack32[...].reshape(GROUPS, CAP, K).astype(BF16)

    pl.semaphore_wait(barrier, GROUPS - 1 + SUBS - 1 + SECT - twin.astype(jnp.int32))

    def five_copy(i):
        rows = five.at[pl.ds(own, 128), :]
        return pltpu.make_async_remote_copy(
            src_ref=rows, dst_ref=rows, send_sem=five_send, recv_sem=five_recv,
            device_id=(g, lax.rem(s + i, SUBS)), device_id_type=MESH,
        )

    for i in range(1, SUBS):
        five_copy(i).start()

    slots[g] = pack[g]

    def send_slot(i, carry):
        j = lax.rem(g + i, GROUPS)
        pltpu.make_async_remote_copy(
            src_ref=pack.at[j], dst_ref=slots.at[g], send_sem=slot_send, recv_sem=slot_recv,
            device_id=(j, s), device_id_type=MESH,
        ).start()
        return carry

    lax.fori_loop(1, GROUPS, send_slot, 0)

    tmp[pl.ds(128, 128), :] = jnp.zeros((128, 128), jnp.int32)
    tmp[pl.ds(0, CLASSES), :] = jnp.where(src5[...] < 0, EMPTY, src5[...])
    idx5[0] = jnp.transpose(tmp[pl.ds(0, 128), :])
    idx5[1] = jnp.transpose(tmp[pl.ds(128, 128), :])
    idx4[0] = src4[:, 0:128]
    idx4[1, :, 0 : CLASSES - 128] = src4[:, 128:CLASSES]
    top = src3[...]
    grp3 = jnp.right_shift(top, 4)
    place = jnp.bitwise_and(grp3, 7) * (16 * SECT) + jnp.right_shift(grp3, 3) * 16 + jnp.bitwise_and(top, 15)
    place = jnp.where(top < 0, -1, place)
    tmp[...] = jnp.zeros((256, 128), jnp.int32)
    tmp[0:2, :] = place[:, 0:128]
    tmp[128:130, 0 : CLASSES - 128] = place[:, 128:CLASSES]
    idx3[0] = jnp.transpose(tmp[pl.ds(0, 128), :])
    idx3[1] = jnp.transpose(tmp[pl.ds(128, 128), :])

    lane = lax.broadcasted_iota(jnp.int32, (128, 256), 1)

    def one_hot(col):
        low = jnp.bitwise_and(col, 255)
        return jnp.where(lane == jnp.concatenate([low, low], 1), 1.0, 0.0).astype(BF16)

    def build(i, carry):
        for q in range(3):
            c = 3 * i + q
            hot5[pl.ds(pl.multiple_of(c * 128, 128), 128), :] = one_hot(column(idx5[c // 128], c % 128))
        return carry

    lax.fori_loop(0, CLASSES // 3, build, 0)
    for t in range(2):
        for h in range(2):
            hot3[pl.ds((2 * t + h) * 128, 128), :] = one_hot(column(idx3[h], t))

    def drain(buffer, count, send, recv):
        part = buffer.at[pl.ds(0, count)]
        return pltpu.make_async_remote_copy(
            src_ref=part, dst_ref=part, send_sem=send, recv_sem=recv, device_id=(g, s), device_id_type=MESH
        )

    drain(five, 7 * 128, five_send, five_recv).wait_recv()
    four = ascend(five[...], 128, wide, up)
    three = ascend(four, 16, wide, up)

    section = pl.multiple_of(s * (16 * SECT), 16)

    held = tops.at[pl.ds(SUBS * 16 * SECT, 16), :]
    tops[pl.ds(SUBS * 16 * SECT, 16), :] = three
    spot = pl.multiple_of(gs * (16 * SECT) + (g // SUBS) * 16, 16)

    @pl.when(twin)
    def _():
        tops[pl.ds(spot, 16), :] = three

    def send_top(m, carry):
        j, other = partner(m)

        @pl.when(other)
        def _():
            pltpu.make_async_remote_copy(
                src_ref=held, dst_ref=tops.at[pl.ds(spot, 16), :], send_sem=top_send, recv_sem=top_recv,
                device_id=(j, gs), device_id_type=MESH,
            ).start()

        return carry

    lax.fori_loop(0, SECT, send_top, 0)

    fetch.wait()

    lane4 = lax.broadcasted_iota(jnp.int32, (16, 128), 1)

    def near(i, total):
        base = i * STEP
        rows = pl.ds(pl.multiple_of(base * 128, 128), STEP * 128)
        hot = hot5[rows, :]
        r0 = mm(hot, jnp.concatenate([five[0:256, :], five[256:512, :]], 1))
        r1 = mm(hot, jnp.concatenate([five[512:768, :], five[768:1024, :]], 1))
        hot4 = []
        for q in range(STEP):
            c = base + q
            hot4.append(jnp.where(lane4 == column(idx4[c // 128], c % 128), 1.0, 0.0))
        r4 = mm(jnp.concatenate(hot4, 0).astype(BF16), four)
        parts = []
        for q in range(STEP):
            c = base + q
            col = column(idx5[c // 128], c % 128)
            odd = jnp.bitwise_and(col, 256) != 0
            upper = jnp.bitwise_and(col, 512) != 0
            a = r0[q * 128 : (q + 1) * 128]
            b = r1[q * 128 : (q + 1) * 128]
            picked = jnp.where(
                upper, jnp.where(odd, b[:, 128:], b[:, :128]), jnp.where(odd, a[:, 128:], a[:, :128])
            )
            picked = jnp.where(col < NEAR, picked, 0.0)
            parts.append(jnp.concatenate([picked, r4[q * 16 : (q + 1) * 16]], 0).astype(BF16))
        weights = ops[pl.ds(base, STEP)].reshape(STEP * 128, K)
        return total + mm(jnp.concatenate(parts, 1), weights)

    half = STEPS // 3
    total = lax.fori_loop(0, half, near, jnp.zeros((144, K), F32))

    @pl.when(twin)
    def _():
        drain(tops, 16 * (SECT - 1), top_send, top_recv).wait_recv()

    @pl.when(jnp.logical_not(twin))
    def _():
        drain(tops, 16 * SECT, top_send, top_recv).wait_recv()

    for i in range(1, SUBS):
        rows = tops.at[pl.ds(section, 16 * SECT), :]
        pltpu.make_async_remote_copy(
            src_ref=rows, dst_ref=rows, send_sem=rest_send, recv_sem=rest_recv,
            device_id=(g, lax.rem(s + i, SUBS)), device_id_type=MESH,
        ).start()

    total = lax.fori_loop(half, STEPS, near, total)

    drain(tops, 7 * 16 * SECT, rest_send, rest_recv).wait_recv()
    drain(slots, GROUPS - 1, slot_send, slot_recv).wait_recv()
    store[0 : GROUPS * CAP, :] = slots[...].astype(F32).reshape(GROUPS * CAP, K).astype(BF16)
    store[GROUPS * CAP : 512, :] = jnp.zeros((512 - GROUPS * CAP, K), BF16)

    picks3[...] = jnp.zeros((2048, K), F32)
    quads = [
        mm(hot3[...], jnp.concatenate([tops[512 * b : 512 * b + 256, :], tops[512 * b + 256 : 512 * b + 512, :]], 1))
        for b in range(3)
    ]
    for t in range(2):
        for h in range(2):
            col = column(idx3[h], t)
            odd = jnp.bitwise_and(col, 256) != 0
            r = [x[(2 * t + h) * 128 : (2 * t + h + 1) * 128] for x in quads]
            r = [jnp.where(odd, x[:, 128:], x[:, :128]) for x in r]
            got = jnp.where(col >= 1024, r[2], jnp.where(col >= 512, r[1], r[0]))
            picks3[pl.ds(1024 * h + t, 128, stride=8), :] = jnp.where(col < 0, 0.0, got)

    def far(i, total):
        base = i * STEP
        rows = pl.ds(pl.multiple_of(base * 128, 128), STEP * 128)
        r = mm(hot5[rows, :], jnp.concatenate([store[0:256, :], store[256:512, :]], 1))
        parts = []
        for q in range(STEP):
            c = base + q
            col = column(idx5[c // 128], c % 128)
            odd = jnp.bitwise_and(col, 256) != 0
            a = r[q * 128 : (q + 1) * 128]
            picked = jnp.where(col < NEAR, 0.0, jnp.where(odd, a[:, 128:], a[:, :128]))
            third = picks3[pl.ds(pl.multiple_of(c * 8, 8), 8), :]
            parts.append(jnp.concatenate([picked, third], 0).astype(BF16))
        weights = ops[pl.ds(base, STEP)].reshape(STEP * 128, K)
        return total + mm(jnp.concatenate(parts, 1), weights)

    rest = lax.fori_loop(0, STEPS, far, jnp.zeros((136, K), F32))

    local = rest[128:136].astype(BF16)
    for c in range(8):
        wide[pl.ds(c, 8, stride=8), :] = mm(local, down[c])
    local = (wide[0:16, :] + total[128:144]).astype(BF16)
    for c in range(8):
        wide[pl.ds(c, 16, stride=8), :] = mm(local, down[c])
    local = (wide[0:128, :] + (total[0:128] + rest[0:128])).astype(BF16)
    for c in range(8):
        out[pl.ds(c, 128, stride=8), :] = mm(local, down[c])

    for i in range(1, SUBS):
        five_copy(i).wait_send()
    drain(slots, GROUPS - 1, slot_send, slot_recv).wait_send()

    @pl.when(twin)
    def _():
        drain(tops, 16 * (SECT - 1), top_send, top_recv).wait_send()

    @pl.when(jnp.logical_not(twin))
    def _():
        drain(tops, 16 * SECT, top_send, top_recv).wait_send()

    drain(tops, 7 * 16 * SECT, rest_send, rest_recv).wait_send()


def body(multipoles, up_ops, down_ops, far_ops, sources5, sources4, sources3, send_boxes, send_counts):
    vmem = pl.BlockSpec(memory_space=pltpu.VMEM)
    dma = pltpu.SemaphoreType.DMA
    return pl.pallas_call(
        kernel,
        out_shape=jax.ShapeDtypeStruct((1024, K), F32),
        in_specs=[vmem] * 8 + [pl.BlockSpec(memory_space=pl.ANY)],
        out_specs=vmem,
        scratch_shapes=[
            pltpu.VMEM((NEAR, K), BF16),
            pltpu.VMEM((GROUPS * CAP, K), F32),
            pltpu.VMEM((GROUPS, CAP, K), BF16),
            pltpu.VMEM((GROUPS, CAP, K), BF16),
            pltpu.VMEM((512, K), BF16),
            pltpu.VMEM((SUBS * 16 * SECT + 16, K), BF16),
            pltpu.VMEM((CLASSES, K, K), BF16),
            pltpu.VMEM((CLASSES * 128, 256), BF16),
            pltpu.VMEM((512, 256), BF16),
            pltpu.VMEM((2, 128, 128), jnp.int32),
            pltpu.VMEM((2, 16, 128), jnp.int32),
            pltpu.VMEM((2, 128, 128), jnp.int32),
            pltpu.VMEM((256, 128), jnp.int32),
            pltpu.VMEM((1024, K), F32),
            pltpu.VMEM((2048, K), F32),
        ]
        + [dma] * 9,
        compiler_params=pltpu.CompilerParams(
            collective_id=0, has_side_effects=True, vmem_limit_bytes=48 * 2**20
        ),
    )(
        multipoles, up_ops, down_ops, sources5, sources4.T, sources3.T, send_boxes[0].T, send_counts, far_ops
    )


def solution(mesh):
    in_specs = (
        P(("grp", "sub"), None),
        P(),
        P(),
        P(),
        P(None, ("grp", "sub")),
        P(None, ("grp", "sub")),
        P(None, ("grp", "sub")),
        P(("grp", "sub"), None, None),
        P(("grp", "sub"), None),
    )
    out_specs = P(("grp", "sub"), None)
    return jax.shard_map(body, mesh=mesh, in_specs=in_specs, out_specs=out_specs, check_vma=False)
```

```python
import functools

import jax
import jax.numpy as jnp
from jax import lax
from jax.experimental import pallas as pl
from jax.experimental.pallas import tpu as pltpu
from jax.sharding import PartitionSpec as P

K = 128
CLASSES = 189
CAP = 4
GROUPS = 96
SUBS = 8
SIDE = 8
RING = GROUPS // SIDE
MESSAGE = 8
SECT = 2 * GROUPS
NEAR = 1024
EMPTY = 1535
STEP = 63
BUILD = 63
STEPS = CLASSES // STEP
MESH = pl.DeviceIdType.MESH
F32 = jnp.float32
BF16 = jnp.bfloat16


def mm(a, b):
    return jnp.dot(a, b, preferred_element_type=F32)


def ascend(rows, count, wide, up):
    wide[pl.ds(0, 8 * count), :] = rows.astype(F32)
    total = jnp.zeros((count, K), F32)
    for c in range(8):
        total += mm(wide[pl.ds(c, count, stride=8), :].astype(BF16), up[c])
    return total.astype(BF16)


def column(block, c):
    return jnp.take_along_axis(block, jnp.full(block.shape, c, jnp.int32), axis=1)


def kernel(
    mult_hbm, up_hbm, down_hbm, src5_hbm, src4_hbm, src3_hbm, boxes_hbm, counts_hbm, ops_hbm, out,
    mult, up, down, src5, src4, src3, boxes, counts, ops,
    five, pack32, pack, slots, store, tops, hot5, hot3, picks0, picks1, picks2, picks43, idx5, low5, idx4, idx3, tmp, wide, picks3,
    in_sems, five_send, five_recv, slot_send, slot_recv, rest_send, rest_recv,
):
    g = lax.axis_index("grp")
    s = lax.axis_index("sub")

    loads = [
        pltpu.make_async_copy(src, dst, in_sems.at[i])
        for i, (src, dst) in enumerate(
            [
                (mult_hbm, mult), (up_hbm, up), (boxes_hbm, boxes), (counts_hbm, counts), (src5_hbm, src5),
                (src4_hbm, src4), (src3_hbm, src3), (down_hbm, down), (ops_hbm, ops),
            ]
        )
    ]
    for load in loads:
        load.start()

    barrier = pltpu.get_barrier_semaphore()

    def peer(i):
        kz = i // SIDE
        ky = lax.rem(i, SIDE)
        dz = RING // 2 + ((kz + 1) // 2) * (1 - 2 * lax.rem(kz, 2))
        dy = SIDE // 2 + ((ky + 1) // 2) * (1 - 2 * lax.rem(ky, 2))
        return lax.rem(g // RING + dy, SIDE) * RING + lax.rem(lax.rem(g, RING) + dz, RING)

    def greet(i, carry):
        pl.semaphore_signal(barrier, inc=1, device_id=(peer(i), s), device_id_type=MESH)
        return carry

    lax.fori_loop(0, GROUPS - 1, greet, 0)
    for i in range(1, SUBS):
        pl.semaphore_signal(barrier, inc=1, device_id=(g, lax.rem(s + i, SUBS)), device_id_type=MESH)

    loads[0].wait()
    loads[1].wait()
    mine = ascend(mult[...], 128, wide, up)
    own = pl.multiple_of(s * 128, 128)
    five[pl.ds(own, 128), :] = mine
    top = ascend(ascend(mine, 16, wide, up), 2, wide, up).astype(F32)

    loads[2].wait()
    loads[3].wait()
    box = lax.broadcasted_iota(jnp.int32, (128, GROUPS), 0)
    for k in range(CAP):
        hit = jnp.logical_and(box == boxes[k : k + 1, :], counts[...] > k)
        pack32[pl.ds(k, GROUPS, stride=MESSAGE), :] = lax.dot_general(
            jnp.where(hit, 1.0, 0.0).astype(BF16), mine, (((0,), (0,)), ((), ())), preferred_element_type=F32
        )
    for r in range(2):
        pack32[pl.ds(CAP + r, GROUPS, stride=MESSAGE), :] = jnp.broadcast_to(top[r : r + 1], (GROUPS, K))
        pack32[pl.ds(CAP + 2 + r, GROUPS, stride=MESSAGE), :] = jnp.zeros((GROUPS, K), F32)
    pack[...] = pack32[...].reshape(GROUPS, MESSAGE, K).astype(BF16)

    pl.semaphore_wait(barrier, GROUPS - 1 + SUBS - 1)

    def round_group(rows, send, recv):
        return [
            pltpu.make_async_remote_copy(
                src_ref=rows, dst_ref=rows, send_sem=send, recv_sem=recv,
                device_id=(g, lax.rem(s + i, SUBS)), device_id_type=MESH,
            )
            for i in range(1, SUBS)
        ]

    def drain(buffer, count, send, recv):
        part = buffer.at[pl.ds(0, count)]
        return pltpu.make_async_remote_copy(
            src_ref=part, dst_ref=part, send_sem=send, recv_sem=recv, device_id=(g, s), device_id_type=MESH
        )

    for copy in round_group(five.at[pl.ds(own, 128), :], five_send, five_recv):
        copy.start()

    slots[g] = pack[g]

    def send_slot(i, carry):
        j = peer(i)
        pltpu.make_async_remote_copy(
            src_ref=pack.at[j], dst_ref=slots.at[g], send_sem=slot_send, recv_sem=slot_recv,
            device_id=(j, s), device_id_type=MESH,
        ).start()
        return carry

    lax.fori_loop(0, GROUPS - 1, send_slot, 0)

    for load in loads[4:7]:
        load.wait()
    tmp[pl.ds(128, 128), :] = jnp.zeros((128, 128), jnp.int32)
    entry = src5[...]
    slot = entry - NEAR
    slot = NEAR + jnp.bitwise_and(slot, 3) * GROUPS + jnp.right_shift(slot, 2)
    tmp[pl.ds(0, CLASSES), :] = jnp.where(entry < 0, EMPTY, jnp.where(entry < NEAR, entry, slot))
    idx5[0] = jnp.transpose(tmp[pl.ds(0, 128), :])
    idx5[1] = jnp.transpose(tmp[pl.ds(128, 128), :])
    low5[...] = jnp.bitwise_and(idx5[...], 255)
    idx5[...] = jnp.right_shift(idx5[...], 8)
    idx4[0] = src4[:, 0:128]
    idx4[1, :, 0 : CLASSES - 128] = src4[:, 128:CLASSES]
    entry = src3[...]
    place = jnp.bitwise_and(jnp.right_shift(entry, 1), 7) * SECT + jnp.bitwise_and(entry, 1) * GROUPS
    place = jnp.where(entry < 0, -1, place + jnp.right_shift(entry, 4))
    tmp[...] = jnp.zeros((256, 128), jnp.int32)
    tmp[0:2, :] = place[:, 0:128]
    tmp[128:130, 0 : CLASSES - 128] = place[:, 128:CLASSES]
    idx3[0] = jnp.transpose(tmp[pl.ds(0, 128), :])
    idx3[1] = jnp.transpose(tmp[pl.ds(128, 128), :])

    lane = lax.broadcasted_iota(jnp.int32, (128, 256), 1)

    def one_hot(low):
        return jnp.where(lane == jnp.concatenate([low, low], 1), 1.0, 0.0).astype(BF16)

    def build(i, carry):
        for q in range(BUILD):
            c = BUILD * i + q
            hot5[pl.ds(pl.multiple_of(c * 128, 128), 128), :] = one_hot(column(low5[c // 128], c % 128))
        return carry

    lax.fori_loop(0, CLASSES // BUILD, build, 0)
    for t in range(2):
        for h in range(2):
            hot3[pl.ds((2 * t + h) * 128, 128), :] = one_hot(jnp.bitwise_and(column(idx3[h], t), 255))
    picks3[...] = jnp.zeros((2048, K), F32)

    drain(five, 7 * 128, five_send, five_recv).wait_recv()
    four = ascend(five[...], 128, wide, up)
    lane4 = lax.broadcasted_iota(jnp.int32, (16, 128), 1)

    def lanes(c):
        return pl.ds(pl.multiple_of(c * K, K), K)

    def tiles(c, *parts):
        hot = hot5[pl.ds(pl.multiple_of(c * 128, 128), 128), :]
        block = column(idx5[c // 128], c % 128)
        for b, table, picks in parts:
            r = mm(hot, table)
            picked = jnp.where(block == 2 * b, r[:, :K], jnp.where(block == 2 * b + 1, r[:, K:], 0.0))
            picks[:, lanes(c)] = picked.astype(BF16)

    def near(i, carry):
        first = jnp.concatenate([five[0:256, :], five[256:512, :]], 1)
        second = jnp.concatenate([five[512:768, :], five[768:1024, :]], 1)
        base = i * STEP
        hot4 = []
        for q in range(STEP):
            c = base + q
            tiles(c, (0, first, picks0), (1, second, picks1))
            hot4.append(jnp.where(lane4 == column(idx4[c // 128], c % 128), 1.0, 0.0))
        r4 = mm(jnp.concatenate(hot4, 0).astype(BF16), four)
        for q in range(STEP):
            picks43[0:16, lanes(base + q)] = r4[q * 16 : (q + 1) * 16].astype(BF16)
        return carry

    early = CLASSES // STEP - 1
    lax.fori_loop(0, early, near, 0)

    drain(slots, GROUPS - 1, slot_send, slot_recv).wait_recv()
    wide[0 : GROUPS * MESSAGE, :] = slots[...].astype(F32).reshape(GROUPS * MESSAGE, K)
    for k in range(CAP):
        store[k * GROUPS : (k + 1) * GROUPS, :] = wide[pl.ds(k, GROUPS, stride=MESSAGE), :].astype(BF16)
    store[GROUPS * CAP : 512, :] = jnp.zeros((512 - GROUPS * CAP, K), BF16)
    section = pl.multiple_of(s * SECT, SECT)
    for r in range(2):
        tops[pl.ds(pl.multiple_of(section + r * GROUPS, GROUPS), GROUPS), :] = wide[
            pl.ds(CAP + r, GROUPS, stride=MESSAGE), :
        ].astype(BF16)
    for copy in round_group(tops.at[pl.ds(section, SECT), :], rest_send, rest_recv):
        copy.start()

    lax.fori_loop(early, CLASSES // STEP, near, 0)

    def far(i, carry):
        third = jnp.concatenate([store[0:256, :], store[256:512, :]], 1)
        for q in range(STEP):
            tiles(i * STEP + q, (2, third, picks2))
        return carry

    lax.fori_loop(0, CLASSES // STEP, far, 0)

    drain(tops, 7 * SECT, rest_send, rest_recv).wait_recv()
    quads = [
        mm(hot3[...], jnp.concatenate([tops[512 * b : 512 * b + 256, :], tops[512 * b + 256 : 512 * b + 512, :]], 1))
        for b in range(3)
    ]
    for t in range(2):
        for h in range(2):
            col = column(idx3[h], t)
            odd = jnp.bitwise_and(col, 256) != 0
            r = [x[(2 * t + h) * 128 : (2 * t + h + 1) * 128] for x in quads]
            r = [jnp.where(odd, x[:, 128:], x[:, :128]) for x in r]
            got = jnp.where(col >= 1024, r[2], jnp.where(col >= 512, r[1], r[0]))
            picks3[pl.ds(1024 * h + t, 128, stride=8), :] = jnp.where(col < 0, 0.0, got)

    loads[8].wait()

    def apply(i, total):
        base = i * STEP
        for q in range(STEP):
            c = base + q
            rows = picks3[pl.ds(pl.multiple_of(c * 8, 8), 8), :]
            picks43[16:32, lanes(c)] = jnp.concatenate([rows, rows], 0).astype(BF16)
        span = pl.ds(pl.multiple_of(base * K, K), STEP * K)
        picked = jnp.concatenate([picks0[:, span] + picks1[:, span] + picks2[:, span], picks43[:, span]], 0)
        return total + mm(picked, ops[pl.ds(base, STEP)].reshape(STEP * K, K))

    total = lax.fori_loop(0, CLASSES // STEP, apply, jnp.zeros((160, K), F32))

    loads[7].wait()
    local = total[144:152].astype(BF16)
    for c in range(8):
        wide[pl.ds(c, 8, stride=8), :] = mm(local, down[c])
    local = (wide[0:16, :] + total[128:144]).astype(BF16)
    for c in range(8):
        wide[pl.ds(c, 16, stride=8), :] = mm(local, down[c])
    local = (wide[0:128, :] + total[0:128]).astype(BF16)
    for c in range(8):
        out[pl.ds(c, 128, stride=8), :] = mm(local, down[c])

    drain(five, 7 * 128, five_send, five_recv).wait_send()
    drain(slots, GROUPS - 1, slot_send, slot_recv).wait_send()
    drain(tops, 7 * SECT, rest_send, rest_recv).wait_send()


def body(multipoles, up_ops, down_ops, far_ops, sources5, sources4, sources3, send_boxes, send_counts):
    dma = pltpu.SemaphoreType.DMA
    operands = (
        multipoles, up_ops, down_ops, sources5, sources4.T, sources3.T, send_boxes[0].T, send_counts, far_ops
    )
    return pl.pallas_call(
        kernel,
        out_shape=jax.ShapeDtypeStruct((1024, K), F32),
        in_specs=[pl.BlockSpec(memory_space=pl.ANY)] * 9,
        out_specs=pl.BlockSpec(memory_space=pltpu.VMEM),
        scratch_shapes=[pltpu.VMEM(x.shape, x.dtype) for x in operands]
        + [
            pltpu.VMEM((NEAR, K), BF16),
            pltpu.VMEM((GROUPS * MESSAGE, K), F32),
            pltpu.VMEM((GROUPS, MESSAGE, K), BF16),
            pltpu.VMEM((GROUPS, MESSAGE, K), BF16),
            pltpu.VMEM((512, K), BF16),
            pltpu.VMEM((SUBS * SECT, K), BF16),
            pltpu.VMEM((CLASSES * 128, 256), BF16),
            pltpu.VMEM((512, 256), BF16),
            pltpu.VMEM((128, CLASSES * K), BF16),
            pltpu.VMEM((128, CLASSES * K), BF16),
            pltpu.VMEM((128, CLASSES * K), BF16),
            pltpu.VMEM((32, CLASSES * K), BF16),
            pltpu.VMEM((2, 128, 128), jnp.int32),
            pltpu.VMEM((2, 128, 128), jnp.int32),
            pltpu.VMEM((2, 16, 128), jnp.int32),
            pltpu.VMEM((2, 128, 128), jnp.int32),
            pltpu.VMEM((256, 128), jnp.int32),
            pltpu.VMEM((1024, K), F32),
            pltpu.VMEM((2048, K), F32),
            dma((9,)),
        ]
        + [dma] * 6,
        compiler_params=pltpu.CompilerParams(
            collective_id=0, has_side_effects=True, vmem_limit_bytes=56 * 2**20
        ),
    )(*operands)


def solution(mesh):
    in_specs = (
        P(("grp", "sub"), None),
        P(),
        P(),
        P(),
        P(None, ("grp", "sub")),
        P(None, ("grp", "sub")),
        P(None, ("grp", "sub")),
        P(("grp", "sub"), None, None),
        P(("grp", "sub"), None),
    )
    out_specs = P(("grp", "sub"), None)
    return jax.shard_map(body, mesh=mesh, in_specs=in_specs, out_specs=out_specs, check_vma=False)
```

```python
import functools

import jax
import jax.numpy as jnp
from jax import lax
from jax.experimental import pallas as pl
from jax.experimental.pallas import tpu as pltpu
from jax.sharding import PartitionSpec as P

K = 128
CLASSES = 189
CAP = 4
GROUPS = 96
SUBS = 8
SIDE = 8
RING = GROUPS // SIDE
MESSAGE = 8
SECT = 2 * GROUPS
NEAR = 1024
EMPTY = 1535
STEP = 63
BUILD = 63
STEPS = CLASSES // STEP
MESH = pl.DeviceIdType.MESH
F32 = jnp.float32
BF16 = jnp.bfloat16


def mm(a, b):
    return jnp.dot(a, b, preferred_element_type=F32)


def ascend(rows, count, wide, up):
    wide[pl.ds(0, 8 * count), :] = rows.astype(F32)
    total = jnp.zeros((count, K), F32)
    for c in range(8):
        total += mm(wide[pl.ds(c, count, stride=8), :].astype(BF16), up[c])
    return total.astype(BF16)


def column(block, c):
    return jnp.take_along_axis(block, jnp.full(block.shape, c, jnp.int32), axis=1)


def kernel(
    mult_hbm, up_hbm, down_hbm, src5_hbm, src4_hbm, src3_hbm, boxes_hbm, counts_hbm, ops_hbm, out,
    mult, up, down, src5, src4, src3, boxes, counts, ops,
    five, pack32, pack, slots, store, tops, hot5, hot3, picks0, picks1, picks2, picks43, idx5, low5, idx4, idx3, tmp, wide, picks3,
    in_sems, five_send, five_recv, slot_send, slot_recv, rest_send, rest_recv,
):
    g = lax.axis_index("grp")
    s = lax.axis_index("sub")

    loads = [
        pltpu.make_async_copy(src, dst, in_sems.at[i])
        for i, (src, dst) in enumerate(
            [
                (mult_hbm, mult), (up_hbm, up), (boxes_hbm, boxes), (counts_hbm, counts), (src5_hbm, src5),
                (src4_hbm, src4), (src3_hbm, src3), (down_hbm, down), (ops_hbm, ops),
            ]
        )
    ]
    for load in loads:
        load.start()

    barrier = pltpu.get_barrier_semaphore()

    def peer(i):
        kz = i // SIDE
        ky = lax.rem(i, SIDE)
        dz = RING // 2 + ((kz + 1) // 2) * (1 - 2 * lax.rem(kz, 2))
        dy = SIDE // 2 + ((ky + 1) // 2) * (1 - 2 * lax.rem(ky, 2))
        return lax.rem(g // RING + dy, SIDE) * RING + lax.rem(lax.rem(g, RING) + dz, RING)

    def greet(i, carry):
        pl.semaphore_signal(barrier, inc=1, device_id=(peer(i), s), device_id_type=MESH)
        return carry

    lax.fori_loop(0, GROUPS - 1, greet, 0)
    for i in range(1, SUBS):
        pl.semaphore_signal(barrier, inc=1, device_id=(g, lax.rem(s + i, SUBS)), device_id_type=MESH)

    loads[0].wait()
    loads[1].wait()
    mine = ascend(mult[...], 128, wide, up)
    own = pl.multiple_of(s * 128, 128)
    five[pl.ds(own, 128), :] = mine
    top = ascend(ascend(mine, 16, wide, up), 2, wide, up).astype(F32)

    loads[2].wait()
    loads[3].wait()
    box = lax.broadcasted_iota(jnp.int32, (128, GROUPS), 0)
    for k in range(CAP):
        hit = jnp.logical_and(box == boxes[k : k + 1, :], counts[...] > k)
        pack32[pl.ds(k, GROUPS, stride=MESSAGE), :] = lax.dot_general(
            jnp.where(hit, 1.0, 0.0).astype(BF16), mine, (((0,), (0,)), ((), ())), preferred_element_type=F32
        )
    for r in range(2):
        pack32[pl.ds(CAP + r, GROUPS, stride=MESSAGE), :] = jnp.broadcast_to(top[r : r + 1], (GROUPS, K))
        pack32[pl.ds(CAP + 2 + r, GROUPS, stride=MESSAGE), :] = jnp.zeros((GROUPS, K), F32)
    pack[...] = pack32[...].reshape(GROUPS, MESSAGE, K).astype(BF16)

    for load in loads[4:7]:
        load.wait()
    tmp[pl.ds(128, 128), :] = jnp.zeros((128, 128), jnp.int32)
    entry = src5[...]
    slot = entry - NEAR
    slot = NEAR + jnp.bitwise_and(slot, 3) * GROUPS + jnp.right_shift(slot, 2)
    tmp[pl.ds(0, CLASSES), :] = jnp.where(entry < 0, EMPTY, jnp.where(entry < NEAR, entry, slot))
    idx5[0] = jnp.transpose(tmp[pl.ds(0, 128), :])
    idx5[1] = jnp.transpose(tmp[pl.ds(128, 128), :])
    low5[...] = jnp.bitwise_and(idx5[...], 255)
    idx5[...] = jnp.right_shift(idx5[...], 8)
    idx4[0] = src4[:, 0:128]
    idx4[1, :, 0 : CLASSES - 128] = src4[:, 128:CLASSES]
    entry = src3[...]
    place = jnp.bitwise_and(jnp.right_shift(entry, 1), 7) * SECT + jnp.bitwise_and(entry, 1) * GROUPS
    place = jnp.where(entry < 0, -1, place + jnp.right_shift(entry, 4))
    tmp[...] = jnp.zeros((256, 128), jnp.int32)
    tmp[0:2, :] = place[:, 0:128]
    tmp[128:130, 0 : CLASSES - 128] = place[:, 128:CLASSES]
    idx3[0] = jnp.transpose(tmp[pl.ds(0, 128), :])
    idx3[1] = jnp.transpose(tmp[pl.ds(128, 128), :])

    lane = lax.broadcasted_iota(jnp.int32, (128, 256), 1)

    def one_hot(low):
        return jnp.where(lane == jnp.concatenate([low, low], 1), 1.0, 0.0).astype(BF16)

    def build(i, carry):
        for q in range(BUILD):
            c = BUILD * i + q
            hot5[pl.ds(pl.multiple_of(c * 128, 128), 128), :] = one_hot(column(low5[c // 128], c % 128))
        return carry

    lax.fori_loop(0, CLASSES // BUILD, build, 0)
    for t in range(2):
        for h in range(2):
            hot3[pl.ds((2 * t + h) * 128, 128), :] = one_hot(jnp.bitwise_and(column(idx3[h], t), 255))
    picks3[...] = jnp.zeros((2048, K), F32)

    pl.semaphore_wait(barrier, GROUPS - 1 + SUBS - 1)

    def round_group(rows, send, recv):
        return [
            pltpu.make_async_remote_copy(
                src_ref=rows, dst_ref=rows, send_sem=send, recv_sem=recv,
                device_id=(g, lax.rem(s + i, SUBS)), device_id_type=MESH,
            )
            for i in range(1, SUBS)
        ]

    def drain(buffer, count, send, recv):
        part = buffer.at[pl.ds(0, count)]
        return pltpu.make_async_remote_copy(
            src_ref=part, dst_ref=part, send_sem=send, recv_sem=recv, device_id=(g, s), device_id_type=MESH
        )

    for copy in round_group(five.at[pl.ds(own, 128), :], five_send, five_recv):
        copy.start()

    slots[g] = pack[g]

    def send_slot(i, carry):
        j = peer(i)
        pltpu.make_async_remote_copy(
            src_ref=pack.at[j], dst_ref=slots.at[g], send_sem=slot_send, recv_sem=slot_recv,
            device_id=(j, s), device_id_type=MESH,
        ).start()
        return carry

    lax.fori_loop(0, GROUPS - 1, send_slot, 0)

    drain(five, 7 * 128, five_send, five_recv).wait_recv()
    four = ascend(five[...], 128, wide, up)
    lane4 = lax.broadcasted_iota(jnp.int32, (16, 128), 1)

    def lanes(c):
        return pl.ds(pl.multiple_of(c * K, K), K)

    def tiles(c, *parts):
        hot = hot5[pl.ds(pl.multiple_of(c * 128, 128), 128), :]
        block = column(idx5[c // 128], c % 128)
        for b, table, picks in parts:
            r = mm(hot, table)
            picked = jnp.where(block == 2 * b, r[:, :K], jnp.where(block == 2 * b + 1, r[:, K:], 0.0))
            picks[:, lanes(c)] = picked.astype(BF16)

    def near(i, carry):
        first = jnp.concatenate([five[0:256, :], five[256:512, :]], 1)
        second = jnp.concatenate([five[512:768, :], five[768:1024, :]], 1)
        base = i * STEP
        hot4 = []
        for q in range(STEP):
            c = base + q
            tiles(c, (0, first, picks0), (1, second, picks1))
            hot4.append(jnp.where(lane4 == column(idx4[c // 128], c % 128), 1.0, 0.0))
        r4 = mm(jnp.concatenate(hot4, 0).astype(BF16), four)
        for q in range(STEP):
            picks43[0:16, lanes(base + q)] = r4[q * 16 : (q + 1) * 16].astype(BF16)
        return carry

    early = CLASSES // STEP - 1
    lax.fori_loop(0, early, near, 0)

    drain(slots, GROUPS - 1, slot_send, slot_recv).wait_recv()
    wide[0 : GROUPS * MESSAGE, :] = slots[...].astype(F32).reshape(GROUPS * MESSAGE, K)
    for k in range(CAP):
        store[k * GROUPS : (k + 1) * GROUPS, :] = wide[pl.ds(k, GROUPS, stride=MESSAGE), :].astype(BF16)
    store[GROUPS * CAP : 512, :] = jnp.zeros((512 - GROUPS * CAP, K), BF16)
    section = pl.multiple_of(s * SECT, SECT)
    for r in range(2):
        tops[pl.ds(pl.multiple_of(section + r * GROUPS, GROUPS), GROUPS), :] = wide[
            pl.ds(CAP + r, GROUPS, stride=MESSAGE), :
        ].astype(BF16)
    for copy in round_group(tops.at[pl.ds(section, SECT), :], rest_send, rest_recv):
        copy.start()

    lax.fori_loop(early, CLASSES // STEP, near, 0)

    def far(i, carry):
        third = jnp.concatenate([store[0:256, :], store[256:512, :]], 1)
        for q in range(STEP):
            tiles(i * STEP + q, (2, third, picks2))
        return carry

    lax.fori_loop(0, CLASSES // STEP, far, 0)

    drain(tops, 7 * SECT, rest_send, rest_recv).wait_recv()
    quads = [
        mm(hot3[...], jnp.concatenate([tops[512 * b : 512 * b + 256, :], tops[512 * b + 256 : 512 * b + 512, :]], 1))
        for b in range(3)
    ]
    for t in range(2):
        for h in range(2):
            col = column(idx3[h], t)
            odd = jnp.bitwise_and(col, 256) != 0
            r = [x[(2 * t + h) * 128 : (2 * t + h + 1) * 128] for x in quads]
            r = [jnp.where(odd, x[:, 128:], x[:, :128]) for x in r]
            got = jnp.where(col >= 1024, r[2], jnp.where(col >= 512, r[1], r[0]))
            picks3[pl.ds(1024 * h + t, 128, stride=8), :] = jnp.where(col < 0, 0.0, got)

    loads[8].wait()

    def apply(i, total):
        base = i * STEP
        for q in range(STEP):
            c = base + q
            rows = picks3[pl.ds(pl.multiple_of(c * 8, 8), 8), :]
            picks43[16:32, lanes(c)] = jnp.concatenate([rows, rows], 0).astype(BF16)
        span = pl.ds(pl.multiple_of(base * K, K), STEP * K)
        picked = jnp.concatenate([picks0[:, span] + picks1[:, span] + picks2[:, span], picks43[:, span]], 0)
        return total + mm(picked, ops[pl.ds(base, STEP)].reshape(STEP * K, K))

    total = lax.fori_loop(0, CLASSES // STEP, apply, jnp.zeros((160, K), F32))

    loads[7].wait()
    local = total[144:152].astype(BF16)
    for c in range(8):
        wide[pl.ds(c, 8, stride=8), :] = mm(local, down[c])
    local = (wide[0:16, :] + total[128:144]).astype(BF16)
    for c in range(8):
        wide[pl.ds(c, 16, stride=8), :] = mm(local, down[c])
    local = (wide[0:128, :] + total[0:128]).astype(BF16)
    for c in range(8):
        out[pl.ds(c, 128, stride=8), :] = mm(local, down[c])

    drain(five, 7 * 128, five_send, five_recv).wait_send()
    drain(slots, GROUPS - 1, slot_send, slot_recv).wait_send()
    drain(tops, 7 * SECT, rest_send, rest_recv).wait_send()


def body(multipoles, up_ops, down_ops, far_ops, sources5, sources4, sources3, send_boxes, send_counts):
    dma = pltpu.SemaphoreType.DMA
    operands = (
        multipoles, up_ops, down_ops, sources5, sources4.T, sources3.T, send_boxes[0].T, send_counts, far_ops
    )
    return pl.pallas_call(
        kernel,
        out_shape=jax.ShapeDtypeStruct((1024, K), F32),
        in_specs=[pl.BlockSpec(memory_space=pl.ANY)] * 9,
        out_specs=pl.BlockSpec(memory_space=pltpu.VMEM),
        scratch_shapes=[pltpu.VMEM(x.shape, x.dtype) for x in operands]
        + [
            pltpu.VMEM((NEAR, K), BF16),
            pltpu.VMEM((GROUPS * MESSAGE, K), F32),
            pltpu.VMEM((GROUPS, MESSAGE, K), BF16),
            pltpu.VMEM((GROUPS, MESSAGE, K), BF16),
            pltpu.VMEM((512, K), BF16),
            pltpu.VMEM((SUBS * SECT, K), BF16),
            pltpu.VMEM((CLASSES * 128, 256), BF16),
            pltpu.VMEM((512, 256), BF16),
            pltpu.VMEM((128, CLASSES * K), BF16),
            pltpu.VMEM((128, CLASSES * K), BF16),
            pltpu.VMEM((128, CLASSES * K), BF16),
            pltpu.VMEM((32, CLASSES * K), BF16),
            pltpu.VMEM((2, 128, 128), jnp.int32),
            pltpu.VMEM((2, 128, 128), jnp.int32),
            pltpu.VMEM((2, 16, 128), jnp.int32),
            pltpu.VMEM((2, 128, 128), jnp.int32),
            pltpu.VMEM((256, 128), jnp.int32),
            pltpu.VMEM((1024, K), F32),
            pltpu.VMEM((2048, K), F32),
            dma((9,)),
        ]
        + [dma] * 6,
        compiler_params=pltpu.CompilerParams(
            collective_id=0, has_side_effects=True, vmem_limit_bytes=46 * 2**20
        ),
    )(*operands)


def solution(mesh):
    in_specs = (
        P(("grp", "sub"), None),
        P(),
        P(),
        P(),
        P(None, ("grp", "sub")),
        P(None, ("grp", "sub")),
        P(None, ("grp", "sub")),
        P(("grp", "sub"), None, None),
        P(("grp", "sub"), None),
    )
    out_specs = P(("grp", "sub"), None)
    return jax.shard_map(body, mesh=mesh, in_specs=in_specs, out_specs=out_specs, check_vma=False)
```

```python
import functools

import jax
import jax.numpy as jnp
from jax import lax
from jax.experimental import pallas as pl
from jax.experimental.pallas import tpu as pltpu
from jax.sharding import PartitionSpec as P

K = 128
CLASSES = 189
CAP = 4
GROUPS = 96
SUBS = 8
SIDE = 8
RING = GROUPS // SIDE
MESSAGE = 8
SECT = 2 * GROUPS
NEAR = 1024
EMPTY = 1535
STEP = 63
BUILD = 63
STEPS = CLASSES // STEP
MESH = pl.DeviceIdType.MESH
F32 = jnp.float32
BF16 = jnp.bfloat16


def mm(a, b):
    return jnp.dot(a, b, preferred_element_type=F32)


def ascend(rows, count, wide, up):
    wide[pl.ds(0, 8 * count), :] = rows.astype(F32)
    total = jnp.zeros((count, K), F32)
    for c in range(8):
        total += mm(wide[pl.ds(c, count, stride=8), :].astype(BF16), up[c])
    return total.astype(BF16)


def column(block, c):
    return jnp.take_along_axis(block, jnp.full(block.shape, c, jnp.int32), axis=1)


def kernel(
    mult_hbm, up_hbm, down_hbm, src5_hbm, src4_hbm, src3_hbm, boxes_hbm, counts_hbm, ops_hbm, out,
    mult, up, down, src5, src4, src3, boxes, counts, ops,
    five, pack32, pack, slots, store, tops, hot5, hot3, picks0, picks1, picks2, picks43, idx5, low5, idx4, idx3, tmp, wide, picks3,
    in_sems, five_send, five_recv, slot_send, slot_recv, rest_send, rest_recv,
):
    g = lax.axis_index("grp")
    s = lax.axis_index("sub")

    loads = [
        pltpu.make_async_copy(src, dst, in_sems.at[i])
        for i, (src, dst) in enumerate(
            [
                (mult_hbm, mult), (up_hbm, up), (boxes_hbm, boxes), (counts_hbm, counts), (src5_hbm, src5),
                (src4_hbm, src4), (src3_hbm, src3), (down_hbm, down), (ops_hbm, ops),
            ]
        )
    ]
    for load in loads:
        load.start()

    barrier = pltpu.get_barrier_semaphore()

    def peer(i):
        kz = i // SIDE
        ky = lax.rem(i, SIDE)
        dz = RING // 2 + ((kz + 1) // 2) * (1 - 2 * lax.rem(kz, 2))
        dy = SIDE // 2 + ((ky + 1) // 2) * (1 - 2 * lax.rem(ky, 2))
        return lax.rem(g // RING + dy, SIDE) * RING + lax.rem(lax.rem(g, RING) + dz, RING)

    def greet(i, carry):
        pl.semaphore_signal(barrier, inc=1, device_id=(peer(i), s), device_id_type=MESH)
        return carry

    lax.fori_loop(0, GROUPS - 1, greet, 0)
    for i in range(1, SUBS):
        pl.semaphore_signal(barrier, inc=1, device_id=(g, lax.rem(s + i, SUBS)), device_id_type=MESH)

    loads[0].wait()
    loads[1].wait()
    mine = ascend(mult[...], 128, wide, up)
    own = pl.multiple_of(s * 128, 128)
    five[pl.ds(own, 128), :] = mine
    top = ascend(ascend(mine, 16, wide, up), 2, wide, up).astype(F32)

    loads[2].wait()
    loads[3].wait()
    box = lax.broadcasted_iota(jnp.int32, (128, GROUPS), 0)
    for k in range(CAP):
        hit = jnp.logical_and(box == boxes[k : k + 1, :], counts[...] > k)
        pack32[pl.ds(k, GROUPS, stride=MESSAGE), :] = lax.dot_general(
            jnp.where(hit, 1.0, 0.0).astype(BF16), mine, (((0,), (0,)), ((), ())), preferred_element_type=F32
        )
    for r in range(2):
        pack32[pl.ds(CAP + r, GROUPS, stride=MESSAGE), :] = jnp.broadcast_to(top[r : r + 1], (GROUPS, K))
        pack32[pl.ds(CAP + 2 + r, GROUPS, stride=MESSAGE), :] = jnp.zeros((GROUPS, K), F32)
    pack[...] = pack32[...].reshape(GROUPS, MESSAGE, K).astype(BF16)

    for load in loads[4:7]:
        load.wait()
    tmp[pl.ds(128, 128), :] = jnp.zeros((128, 128), jnp.int32)
    entry = src5[...]
    slot = entry - NEAR
    slot = NEAR + jnp.bitwise_and(slot, 3) * GROUPS + jnp.right_shift(slot, 2)
    tmp[pl.ds(0, CLASSES), :] = jnp.where(entry < 0, EMPTY, jnp.where(entry < NEAR, entry, slot))
    idx5[0] = jnp.transpose(tmp[pl.ds(0, 128), :])
    idx5[1] = jnp.transpose(tmp[pl.ds(128, 128), :])
    low5[...] = jnp.bitwise_and(idx5[...], 255)
    idx5[...] = jnp.right_shift(idx5[...], 8)
    idx4[0] = src4[:, 0:128]
    idx4[1, :, 0 : CLASSES - 128] = src4[:, 128:CLASSES]
    entry = src3[...]
    place = jnp.bitwise_and(jnp.right_shift(entry, 1), 7) * SECT + jnp.bitwise_and(entry, 1) * GROUPS
    place = jnp.where(entry < 0, -1, place + jnp.right_shift(entry, 4))
    tmp[...] = jnp.zeros((256, 128), jnp.int32)
    tmp[0:2, :] = place[:, 0:128]
    tmp[128:130, 0 : CLASSES - 128] = place[:, 128:CLASSES]
    idx3[0] = jnp.transpose(tmp[pl.ds(0, 128), :])
    idx3[1] = jnp.transpose(tmp[pl.ds(128, 128), :])

    lane = lax.broadcasted_iota(jnp.int32, (128, 256), 1)

    def one_hot(low):
        return jnp.where(lane == jnp.concatenate([low, low], 1), 1.0, 0.0).astype(BF16)

    def build(i, carry):
        for q in range(BUILD):
            c = BUILD * i + q
            hot5[pl.ds(pl.multiple_of(c * 128, 128), 128), :] = one_hot(column(low5[c // 128], c % 128))
        return carry

    lax.fori_loop(0, CLASSES // BUILD, build, 0)
    for t in range(2):
        for h in range(2):
            hot3[pl.ds((2 * t + h) * 128, 128), :] = one_hot(jnp.bitwise_and(column(idx3[h], t), 255))
    picks3[...] = jnp.zeros((2048, K), F32)

    pl.semaphore_wait(barrier, GROUPS - 1 + SUBS - 1)

    def round_group(rows, send, recv):
        return [
            pltpu.make_async_remote_copy(
                src_ref=rows, dst_ref=rows, send_sem=send, recv_sem=recv,
                device_id=(g, lax.rem(s + i, SUBS)), device_id_type=MESH,
            )
            for i in range(1, SUBS)
        ]

    def drain(buffer, count, send, recv):
        part = buffer.at[pl.ds(0, count)]
        return pltpu.make_async_remote_copy(
            src_ref=part, dst_ref=part, send_sem=send, recv_sem=recv, device_id=(g, s), device_id_type=MESH
        )

    for copy in round_group(five.at[pl.ds(own, 128), :], five_send, five_recv):
        copy.start()

    slots[g] = pack[g]

    def send_slot(i, carry):
        j = peer(i)
        pltpu.make_async_remote_copy(
            src_ref=pack.at[j], dst_ref=slots.at[g], send_sem=slot_send, recv_sem=slot_recv,
            device_id=(j, s), device_id_type=MESH,
        ).start()
        return carry

    lax.fori_loop(0, GROUPS - 1, send_slot, 0)

    drain(five, 7 * 128, five_send, five_recv).wait_recv()
    four = ascend(five[...], 128, wide, up)
    lane4 = lax.broadcasted_iota(jnp.int32, (16, 128), 1)

    def lanes(c):
        return pl.ds(pl.multiple_of(c * K, K), K)

    def tiles(c, *parts):
        hot = hot5[pl.ds(pl.multiple_of(c * 128, 128), 128), :]
        block = column(idx5[c // 128], c % 128)
        for b, table, picks in parts:
            r = mm(hot, table)
            picked = jnp.where(block == 2 * b, r[:, :K], jnp.where(block == 2 * b + 1, r[:, K:], 0.0))
            picks[:, lanes(c)] = picked.astype(BF16)

    def near(i, carry):
        first = jnp.concatenate([five[0:256, :], five[256:512, :]], 1)
        second = jnp.concatenate([five[512:768, :], five[768:1024, :]], 1)
        base = i * STEP
        hot4 = []
        for q in range(STEP):
            c = base + q
            tiles(c, (0, first, picks0), (1, second, picks1))
            hot4.append(jnp.where(lane4 == column(idx4[c // 128], c % 128), 1.0, 0.0))
        r4 = mm(jnp.concatenate(hot4, 0).astype(BF16), four)
        for q in range(STEP):
            picks43[0:16, lanes(base + q)] = r4[q * 16 : (q + 1) * 16].astype(BF16)
        return carry

    early = CLASSES // STEP - 1
    lax.fori_loop(0, early, near, 0)

    drain(slots, GROUPS - 1, slot_send, slot_recv).wait_recv()
    wide[0 : GROUPS * MESSAGE, :] = slots[...].astype(F32).reshape(GROUPS * MESSAGE, K)
    for k in range(CAP):
        store[k * GROUPS : (k + 1) * GROUPS, :] = wide[pl.ds(k, GROUPS, stride=MESSAGE), :].astype(BF16)
    store[GROUPS * CAP : 512, :] = jnp.zeros((512 - GROUPS * CAP, K), BF16)
    section = pl.multiple_of(s * SECT, SECT)
    for r in range(2):
        tops[pl.ds(pl.multiple_of(section + r * GROUPS, GROUPS), GROUPS), :] = wide[
            pl.ds(CAP + r, GROUPS, stride=MESSAGE), :
        ].astype(BF16)
    for copy in round_group(tops.at[pl.ds(section, SECT), :], rest_send, rest_recv):
        copy.start()

    lax.fori_loop(early, CLASSES // STEP, near, 0)

    def far(i, carry):
        third = jnp.concatenate([store[0:256, :], store[256:512, :]], 1)
        for q in range(STEP):
            tiles(i * STEP + q, (2, third, picks2))
        return carry

    lax.fori_loop(0, CLASSES // STEP, far, 0)

    drain(tops, 7 * SECT, rest_send, rest_recv).wait_recv()
    quads = [
        mm(hot3[...], jnp.concatenate([tops[512 * b : 512 * b + 256, :], tops[512 * b + 256 : 512 * b + 512, :]], 1))
        for b in range(3)
    ]
    for t in range(2):
        for h in range(2):
            col = column(idx3[h], t)
            odd = jnp.bitwise_and(col, 256) != 0
            r = [x[(2 * t + h) * 128 : (2 * t + h + 1) * 128] for x in quads]
            r = [jnp.where(odd, x[:, 128:], x[:, :128]) for x in r]
            got = jnp.where(col >= 1024, r[2], jnp.where(col >= 512, r[1], r[0]))
            picks3[pl.ds(1024 * h + t, 128, stride=8), :] = jnp.where(col < 0, 0.0, got)

    loads[8].wait()

    def apply(i, total):
        base = i * STEP
        for q in range(STEP):
            c = base + q
            rows = picks3[pl.ds(pl.multiple_of(c * 8, 8), 8), :]
            picks43[16:32, lanes(c)] = jnp.concatenate([rows, rows], 0).astype(BF16)
        span = pl.ds(pl.multiple_of(base * K, K), STEP * K)
        picked = jnp.concatenate([picks0[:, span] + picks1[:, span] + picks2[:, span], picks43[:, span]], 0)
        return total + mm(picked, ops[pl.ds(base, STEP)].reshape(STEP * K, K))

    total = lax.fori_loop(0, CLASSES // STEP, apply, jnp.zeros((160, K), F32))

    loads[7].wait()
    local = total[144:152].astype(BF16)
    for c in range(8):
        wide[pl.ds(c, 8, stride=8), :] = mm(local, down[c])
    local = (wide[0:16, :] + total[128:144]).astype(BF16)
    for c in range(8):
        wide[pl.ds(c, 16, stride=8), :] = mm(local, down[c])
    local = (wide[0:128, :] + total[0:128]).astype(BF16)
    for c in range(8):
        out[pl.ds(c, 128, stride=8), :] = mm(local, down[c])

    drain(five, 7 * 128, five_send, five_recv).wait_send()
    drain(slots, GROUPS - 1, slot_send, slot_recv).wait_send()
    drain(tops, 7 * SECT, rest_send, rest_recv).wait_send()


def body(multipoles, up_ops, down_ops, far_ops, sources5, sources4, sources3, send_boxes, send_counts):
    dma = pltpu.SemaphoreType.DMA
    operands = (
        multipoles, up_ops, down_ops, sources5, sources4.T, sources3.T, send_boxes[0].T, send_counts, far_ops
    )
    return pl.pallas_call(
        kernel,
        out_shape=pltpu.VMEM((1024, K), F32),
        in_specs=[pl.BlockSpec(memory_space=pl.ANY)] * 9,
        out_specs=pl.BlockSpec(memory_space=pltpu.VMEM),
        scratch_shapes=[pltpu.VMEM(x.shape, x.dtype) for x in operands]
        + [
            pltpu.VMEM((NEAR, K), BF16),
            pltpu.VMEM((GROUPS * MESSAGE, K), F32),
            pltpu.VMEM((GROUPS, MESSAGE, K), BF16),
            pltpu.VMEM((GROUPS, MESSAGE, K), BF16),
            pltpu.VMEM((512, K), BF16),
            pltpu.VMEM((SUBS * SECT, K), BF16),
            pltpu.VMEM((CLASSES * 128, 256), BF16),
            pltpu.VMEM((512, 256), BF16),
            pltpu.VMEM((128, CLASSES * K), BF16),
            pltpu.VMEM((128, CLASSES * K), BF16),
            pltpu.VMEM((128, CLASSES * K), BF16),
            pltpu.VMEM((32, CLASSES * K), BF16),
            pltpu.VMEM((2, 128, 128), jnp.int32),
            pltpu.VMEM((2, 128, 128), jnp.int32),
            pltpu.VMEM((2, 16, 128), jnp.int32),
            pltpu.VMEM((2, 128, 128), jnp.int32),
            pltpu.VMEM((256, 128), jnp.int32),
            pltpu.VMEM((1024, K), F32),
            pltpu.VMEM((2048, K), F32),
            dma((9,)),
        ]
        + [dma] * 6,
        compiler_params=pltpu.CompilerParams(
            collective_id=0, has_side_effects=True, vmem_limit_bytes=55 * 2**20
        ),
    )(*operands)


def solution(mesh):
    in_specs = (
        P(("grp", "sub"), None),
        P(),
        P(),
        P(),
        P(None, ("grp", "sub")),
        P(None, ("grp", "sub")),
        P(None, ("grp", "sub")),
        P(("grp", "sub"), None, None),
        P(("grp", "sub"), None),
    )
    out_specs = P(("grp", "sub"), None)
    return jax.shard_map(body, mesh=mesh, in_specs=in_specs, out_specs=out_specs, check_vma=False)
```

```python
import functools

import jax
import jax.numpy as jnp
from jax import lax
from jax.experimental import pallas as pl
from jax.experimental.pallas import tpu as pltpu
from jax.sharding import PartitionSpec as P

K = 128
CLASSES = 189
CAP = 4
GROUPS = 96
SUBS = 8
SIDE = 8
RING = GROUPS // SIDE
MESSAGE = 8
SECT = 2 * GROUPS
NEAR = 1024
EMPTY = 1535
STEP = 63
SENDS = 5
BUILD = 10
STEPS = CLASSES // STEP
MESH = pl.DeviceIdType.MESH
F32 = jnp.float32
BF16 = jnp.bfloat16


def mm(a, b):
    return jnp.dot(a, b, preferred_element_type=F32)


def ascend(rows, count, wide, up):
    wide[pl.ds(0, 8 * count), :] = rows.astype(F32)
    total = jnp.zeros((count, K), F32)
    for c in range(8):
        total += mm(wide[pl.ds(c, count, stride=8), :].astype(BF16), up[c])
    return total.astype(BF16)


def column(block, c):
    return jnp.take_along_axis(block, jnp.full(block.shape, c, jnp.int32), axis=1)


def kernel(
    mult_hbm, up_hbm, down_hbm, src5_hbm, src4_hbm, src3_hbm, boxes_hbm, counts_hbm, ops_hbm, out,
    mult, up, down, src5, src4, src3, boxes, counts, ops,
    five, pack32, pack, slots, store, tops, hot5, hot3, picks0, picks1, picks2, picks43, idx5, low5, idx4, idx3, tmp, wide, picks3,
    in_sems, five_send, five_recv, slot_send, slot_recv, rest_send, rest_recv,
):
    g = lax.axis_index("grp")
    s = lax.axis_index("sub")

    loads = [
        pltpu.make_async_copy(src, dst, in_sems.at[i])
        for i, (src, dst) in enumerate(
            [
                (mult_hbm, mult), (up_hbm, up), (boxes_hbm, boxes), (counts_hbm, counts), (src5_hbm, src5),
                (src4_hbm, src4), (src3_hbm, src3), (down_hbm, down), (ops_hbm, ops),
            ]
        )
    ]
    for load in loads:
        load.start()

    barrier = pltpu.get_barrier_semaphore()

    def peer(i):
        kz = i // SIDE
        ky = lax.rem(i, SIDE)
        dz = RING // 2 + ((kz + 1) // 2) * (1 - 2 * lax.rem(kz, 2))
        dy = SIDE // 2 + ((ky + 1) // 2) * (1 - 2 * lax.rem(ky, 2))
        return lax.rem(g // RING + dy, SIDE) * RING + lax.rem(lax.rem(g, RING) + dz, RING)

    def greet(i, carry):
        pl.semaphore_signal(barrier, inc=1, device_id=(peer(i), s), device_id_type=MESH)
        return carry

    lax.fori_loop(0, GROUPS - 1, greet, 0)
    for i in range(1, SUBS):
        pl.semaphore_signal(barrier, inc=1, device_id=(g, lax.rem(s + i, SUBS)), device_id_type=MESH)

    loads[0].wait()
    loads[1].wait()
    mine = ascend(mult[...], 128, wide, up)
    own = pl.multiple_of(s * 128, 128)
    five[pl.ds(own, 128), :] = mine
    top = ascend(ascend(mine, 16, wide, up), 2, wide, up).astype(F32)

    loads[2].wait()
    loads[3].wait()
    box = lax.broadcasted_iota(jnp.int32, (128, GROUPS), 0)
    for k in range(CAP):
        hit = jnp.logical_and(box == boxes[k : k + 1, :], counts[...] > k)
        pack32[pl.ds(k, GROUPS, stride=MESSAGE), :] = lax.dot_general(
            jnp.where(hit, 1.0, 0.0).astype(BF16), mine, (((0,), (0,)), ((), ())), preferred_element_type=F32
        )
    for r in range(2):
        pack32[pl.ds(CAP + r, GROUPS, stride=MESSAGE), :] = jnp.broadcast_to(top[r : r + 1], (GROUPS, K))
        pack32[pl.ds(CAP + 2 + r, GROUPS, stride=MESSAGE), :] = jnp.zeros((GROUPS, K), F32)
    pack[...] = pack32[...].reshape(GROUPS, MESSAGE, K).astype(BF16)

    for load in loads[4:7]:
        load.wait()
    tmp[pl.ds(128, 128), :] = jnp.zeros((128, 128), jnp.int32)
    entry = src5[...]
    slot = entry - NEAR
    slot = NEAR + jnp.bitwise_and(slot, 3) * GROUPS + jnp.right_shift(slot, 2)
    tmp[pl.ds(0, CLASSES), :] = jnp.where(entry < 0, EMPTY, jnp.where(entry < NEAR, entry, slot))
    idx5[0] = jnp.transpose(tmp[pl.ds(0, 128), :])
    idx5[1] = jnp.transpose(tmp[pl.ds(128, 128), :])
    low5[...] = jnp.bitwise_and(idx5[...], 255)
    idx5[...] = jnp.right_shift(idx5[...], 8)
    idx4[0] = src4[:, 0:128]
    idx4[1, :, 0 : CLASSES - 128] = src4[:, 128:CLASSES]
    entry = src3[...]
    place = jnp.bitwise_and(jnp.right_shift(entry, 1), 7) * SECT + jnp.bitwise_and(entry, 1) * GROUPS
    place = jnp.where(entry < 0, -1, place + jnp.right_shift(entry, 4))
    tmp[...] = jnp.zeros((256, 128), jnp.int32)
    tmp[0:2, :] = place[:, 0:128]
    tmp[128:130, 0 : CLASSES - 128] = place[:, 128:CLASSES]
    idx3[0] = jnp.transpose(tmp[pl.ds(0, 128), :])
    idx3[1] = jnp.transpose(tmp[pl.ds(128, 128), :])

    lane = lax.broadcasted_iota(jnp.int32, (128, 256), 1)

    def one_hot(low):
        return jnp.where(lane == jnp.concatenate([low, low], 1), 1.0, 0.0).astype(BF16)

    pl.semaphore_wait(barrier, GROUPS - 1 + SUBS - 1)

    def round_group(rows, send, recv):
        return [
            pltpu.make_async_remote_copy(
                src_ref=rows, dst_ref=rows, send_sem=send, recv_sem=recv,
                device_id=(g, lax.rem(s + i, SUBS)), device_id_type=MESH,
            )
            for i in range(1, SUBS)
        ]

    def drain(buffer, count, send, recv):
        part = buffer.at[pl.ds(0, count)]
        return pltpu.make_async_remote_copy(
            src_ref=part, dst_ref=part, send_sem=send, recv_sem=recv, device_id=(g, s), device_id_type=MESH
        )

    for copy in round_group(five.at[pl.ds(own, 128), :], five_send, five_recv):
        copy.start()

    slots[g] = pack[g]

    def send_and_build(i, carry):
        for q in range(SENDS):
            j = peer(SENDS * i + q)
            pltpu.make_async_remote_copy(
                src_ref=pack.at[j], dst_ref=slots.at[g], send_sem=slot_send, recv_sem=slot_recv,
                device_id=(j, s), device_id_type=MESH,
            ).start()
        for q in range(BUILD):
            c = BUILD * i + q
            hot5[pl.ds(pl.multiple_of(c * 128, 128), 128), :] = one_hot(column(low5[c // 128], c % 128))
        return carry

    lax.fori_loop(0, (GROUPS - 1) // SENDS, send_and_build, 0)
    for t in range(2):
        for h in range(2):
            hot3[pl.ds((2 * t + h) * 128, 128), :] = one_hot(jnp.bitwise_and(column(idx3[h], t), 255))
    picks3[...] = jnp.zeros((2048, K), F32)

    drain(five, 7 * 128, five_send, five_recv).wait_recv()
    four = ascend(five[...], 128, wide, up)
    lane4 = lax.broadcasted_iota(jnp.int32, (16, 128), 1)

    def lanes(c):
        return pl.ds(pl.multiple_of(c * K, K), K)

    def tiles(c, *parts):
        hot = hot5[pl.ds(pl.multiple_of(c * 128, 128), 128), :]
        block = column(idx5[c // 128], c % 128)
        for b, table, picks in parts:
            r = mm(hot, table)
            picked = jnp.where(block == 2 * b, r[:, :K], jnp.where(block == 2 * b + 1, r[:, K:], 0.0))
            picks[:, lanes(c)] = picked.astype(BF16)

    def near(i, carry):
        first = jnp.concatenate([five[0:256, :], five[256:512, :]], 1)
        second = jnp.concatenate([five[512:768, :], five[768:1024, :]], 1)
        base = i * STEP
        hot4 = []
        for q in range(STEP):
            c = base + q
            tiles(c, (0, first, picks0), (1, second, picks1))
            hot4.append(jnp.where(lane4 == column(idx4[c // 128], c % 128), 1.0, 0.0))
        r4 = mm(jnp.concatenate(hot4, 0).astype(BF16), four)
        for q in range(STEP):
            picks43[0:16, lanes(base + q)] = r4[q * 16 : (q + 1) * 16].astype(BF16)
        return carry

    early = CLASSES // STEP - 1
    lax.fori_loop(0, early, near, 0)

    drain(slots, GROUPS - 1, slot_send, slot_recv).wait_recv()
    wide[0 : GROUPS * MESSAGE, :] = slots[...].astype(F32).reshape(GROUPS * MESSAGE, K)
    for k in range(CAP):
        store[k * GROUPS : (k + 1) * GROUPS, :] = wide[pl.ds(k, GROUPS, stride=MESSAGE), :].astype(BF16)
    store[GROUPS * CAP : 512, :] = jnp.zeros((512 - GROUPS * CAP, K), BF16)
    section = pl.multiple_of(s * SECT, SECT)
    for r in range(2):
        tops[pl.ds(pl.multiple_of(section + r * GROUPS, GROUPS), GROUPS), :] = wide[
            pl.ds(CAP + r, GROUPS, stride=MESSAGE), :
        ].astype(BF16)
    for copy in round_group(tops.at[pl.ds(section, SECT), :], rest_send, rest_recv):
        copy.start()

    lax.fori_loop(early, CLASSES // STEP, near, 0)

    def far(i, carry):
        third = jnp.concatenate([store[0:256, :], store[256:512, :]], 1)
        for q in range(STEP):
            tiles(i * STEP + q, (2, third, picks2))
        return carry

    lax.fori_loop(0, CLASSES // STEP, far, 0)

    drain(tops, 7 * SECT, rest_send, rest_recv).wait_recv()
    quads = [
        mm(hot3[...], jnp.concatenate([tops[512 * b : 512 * b + 256, :], tops[512 * b + 256 : 512 * b + 512, :]], 1))
        for b in range(3)
    ]
    for t in range(2):
        for h in range(2):
            col = column(idx3[h], t)
            odd = jnp.bitwise_and(col, 256) != 0
            r = [x[(2 * t + h) * 128 : (2 * t + h + 1) * 128] for x in quads]
            r = [jnp.where(odd, x[:, 128:], x[:, :128]) for x in r]
            got = jnp.where(col >= 1024, r[2], jnp.where(col >= 512, r[1], r[0]))
            picks3[pl.ds(1024 * h + t, 128, stride=8), :] = jnp.where(col < 0, 0.0, got)

    loads[8].wait()

    def apply(i, total):
        base = i * STEP
        for q in range(STEP):
            c = base + q
            rows = picks3[pl.ds(pl.multiple_of(c * 8, 8), 8), :]
            picks43[16:32, lanes(c)] = jnp.concatenate([rows, rows], 0).astype(BF16)
        span = pl.ds(pl.multiple_of(base * K, K), STEP * K)
        picked = jnp.concatenate([picks0[:, span] + picks1[:, span] + picks2[:, span], picks43[:, span]], 0)
        return total + mm(picked, ops[pl.ds(base, STEP)].reshape(STEP * K, K))

    total = lax.fori_loop(0, CLASSES // STEP, apply, jnp.zeros((160, K), F32))

    loads[7].wait()
    local = total[144:152].astype(BF16)
    for c in range(8):
        wide[pl.ds(c, 8, stride=8), :] = mm(local, down[c])
    local = (wide[0:16, :] + total[128:144]).astype(BF16)
    for c in range(8):
        wide[pl.ds(c, 16, stride=8), :] = mm(local, down[c])
    local = (wide[0:128, :] + total[0:128]).astype(BF16)
    for c in range(8):
        out[pl.ds(c, 128, stride=8), :] = mm(local, down[c])

    drain(five, 7 * 128, five_send, five_recv).wait_send()
    drain(slots, GROUPS - 1, slot_send, slot_recv).wait_send()
    drain(tops, 7 * SECT, rest_send, rest_recv).wait_send()


def body(multipoles, up_ops, down_ops, far_ops, sources5, sources4, sources3, send_boxes, send_counts):
    dma = pltpu.SemaphoreType.DMA
    operands = (
        multipoles, up_ops, down_ops, sources5, sources4.T, sources3.T, send_boxes[0].T, send_counts, far_ops
    )
    return pl.pallas_call(
        kernel,
        out_shape=pltpu.VMEM((1024, K), F32),
        in_specs=[pl.BlockSpec(memory_space=pl.ANY)] * 9,
        out_specs=pl.BlockSpec(memory_space=pltpu.VMEM),
        scratch_shapes=[pltpu.VMEM(x.shape, x.dtype) for x in operands]
        + [
            pltpu.VMEM((NEAR, K), BF16),
            pltpu.VMEM((GROUPS * MESSAGE, K), F32),
            pltpu.VMEM((GROUPS, MESSAGE, K), BF16),
            pltpu.VMEM((GROUPS, MESSAGE, K), BF16),
            pltpu.VMEM((512, K), BF16),
            pltpu.VMEM((SUBS * SECT, K), BF16),
            pltpu.VMEM(((CLASSES + 1) * 128, 256), BF16),
            pltpu.VMEM((512, 256), BF16),
            pltpu.VMEM((128, CLASSES * K), BF16),
            pltpu.VMEM((128, CLASSES * K), BF16),
            pltpu.VMEM((128, CLASSES * K), BF16),
            pltpu.VMEM((32, CLASSES * K), BF16),
            pltpu.VMEM((2, 128, 128), jnp.int32),
            pltpu.VMEM((2, 128, 128), jnp.int32),
            pltpu.VMEM((2, 16, 128), jnp.int32),
            pltpu.VMEM((2, 128, 128), jnp.int32),
            pltpu.VMEM((256, 128), jnp.int32),
            pltpu.VMEM((1024, K), F32),
            pltpu.VMEM((2048, K), F32),
            dma((9,)),
        ]
        + [dma] * 6,
        compiler_params=pltpu.CompilerParams(
            collective_id=0, has_side_effects=True, vmem_limit_bytes=55 * 2**20
        ),
    )(*operands)


def solution(mesh):
    in_specs = (
        P(("grp", "sub"), None),
        P(),
        P(),
        P(),
        P(None, ("grp", "sub")),
        P(None, ("grp", "sub")),
        P(None, ("grp", "sub")),
        P(("grp", "sub"), None, None),
        P(("grp", "sub"), None),
    )
    out_specs = P(("grp", "sub"), None)
    return jax.shard_map(body, mesh=mesh, in_specs=in_specs, out_specs=out_specs, check_vma=False)
```

```python
import functools

import jax
import jax.numpy as jnp
from jax import lax
from jax.experimental import pallas as pl
from jax.experimental.pallas import tpu as pltpu
from jax.sharding import PartitionSpec as P

K = 128
CLASSES = 189
CAP = 4
GROUPS = 96
SUBS = 8
SIDE = 8
RING = GROUPS // SIDE
MESSAGE = 8
SECT = 2 * GROUPS
NEAR = 1024
EMPTY = 1535
STEP = 63
SENDS = 5
BUILD = 10
STEPS = CLASSES // STEP
MESH = pl.DeviceIdType.MESH
F32 = jnp.float32
BF16 = jnp.bfloat16


def mm(a, b):
    return jnp.dot(a, b, preferred_element_type=F32)


def ascend(rows, count, wide, up):
    wide[pl.ds(0, 8 * count), :] = rows.astype(F32)
    total = jnp.zeros((count, K), F32)
    for c in range(8):
        total += mm(wide[pl.ds(c, count, stride=8), :].astype(BF16), up[c])
    return total.astype(BF16)


def column(block, c):
    return jnp.take_along_axis(block, jnp.full(block.shape, c, jnp.int32), axis=1)


def kernel(
    mult_hbm, up_hbm, down_hbm, src5_hbm, src4_hbm, src3_hbm, boxes_hbm, counts_hbm, ops_hbm, out,
    mult, up, down, src5, src4, src3, boxes, counts, ops,
    five, pack32, pack, slots, store, tops, hot5, hot3, picks0, picks1, picks2, picks43, idx5, low5, idx4, idx3, tmp, wide, picks3,
    in_sems, five_send, five_recv, slot_send, slot_recv, rest_send, rest_recv,
):
    g = lax.axis_index("grp")
    s = lax.axis_index("sub")

    loads = [
        pltpu.make_async_copy(src, dst, in_sems.at[i])
        for i, (src, dst) in enumerate(
            [
                (mult_hbm, mult), (up_hbm, up), (boxes_hbm, boxes), (counts_hbm, counts), (src5_hbm, src5),
                (src4_hbm, src4), (src3_hbm, src3), (down_hbm, down), (ops_hbm, ops),
            ]
        )
    ]
    for load in loads:
        load.start()

    barrier = pltpu.get_barrier_semaphore()

    def peer(i):
        kz = i // SIDE
        ky = lax.rem(i, SIDE)
        dz = RING // 2 + ((kz + 1) // 2) * (1 - 2 * lax.rem(kz, 2))
        dy = SIDE // 2 + ((ky + 1) // 2) * (1 - 2 * lax.rem(ky, 2))
        return lax.rem(g // RING + dy, SIDE) * RING + lax.rem(lax.rem(g, RING) + dz, RING)

    def greet(i, carry):
        pl.semaphore_signal(barrier, inc=1, device_id=(peer(i), s), device_id_type=MESH)
        return carry

    lax.fori_loop(0, GROUPS - 1, greet, 0)
    for i in range(1, SUBS):
        pl.semaphore_signal(barrier, inc=1, device_id=(g, lax.rem(s + i, SUBS)), device_id_type=MESH)

    loads[0].wait()
    loads[1].wait()
    mine = ascend(mult[...], 128, wide, up)
    own = pl.multiple_of(s * 128, 128)
    five[pl.ds(own, 128), :] = mine
    top = ascend(ascend(mine, 16, wide, up), 2, wide, up).astype(F32)

    loads[2].wait()
    loads[3].wait()
    box = lax.broadcasted_iota(jnp.int32, (128, GROUPS), 0)
    for k in range(CAP):
        hit = jnp.logical_and(box == boxes[k : k + 1, :], counts[...] > k)
        pack32[pl.ds(k, GROUPS, stride=MESSAGE), :] = lax.dot_general(
            jnp.where(hit, 1.0, 0.0).astype(BF16), mine, (((0,), (0,)), ((), ())), preferred_element_type=F32
        )
    for r in range(2):
        pack32[pl.ds(CAP + r, GROUPS, stride=MESSAGE), :] = jnp.broadcast_to(top[r : r + 1], (GROUPS, K))
        pack32[pl.ds(CAP + 2 + r, GROUPS, stride=MESSAGE), :] = jnp.zeros((GROUPS, K), F32)
    pack[...] = pack32[...].reshape(GROUPS, MESSAGE, K).astype(BF16)

    for load in loads[4:7]:
        load.wait()
    tmp[pl.ds(128, 128), :] = jnp.zeros((128, 128), jnp.int32)
    entry = src5[...]
    slot = entry - NEAR
    slot = NEAR + jnp.bitwise_and(slot, 3) * GROUPS + jnp.right_shift(slot, 2)
    tmp[pl.ds(0, CLASSES), :] = jnp.where(entry < 0, EMPTY, jnp.where(entry < NEAR, entry, slot))
    idx5[0] = jnp.transpose(tmp[pl.ds(0, 128), :])
    idx5[1] = jnp.transpose(tmp[pl.ds(128, 128), :])
    low5[...] = jnp.bitwise_and(idx5[...], 255)
    idx5[...] = jnp.right_shift(idx5[...], 8)
    idx4[0] = src4[:, 0:128]
    idx4[1, :, 0 : CLASSES - 128] = src4[:, 128:CLASSES]
    entry = src3[...]
    place = jnp.bitwise_and(jnp.right_shift(entry, 1), 7) * SECT + jnp.bitwise_and(entry, 1) * GROUPS
    place = jnp.where(entry < 0, -1, place + jnp.right_shift(entry, 4))
    tmp[...] = jnp.zeros((256, 128), jnp.int32)
    tmp[0:2, :] = place[:, 0:128]
    tmp[128:130, 0 : CLASSES - 128] = place[:, 128:CLASSES]
    idx3[0] = jnp.transpose(tmp[pl.ds(0, 128), :])
    idx3[1] = jnp.transpose(tmp[pl.ds(128, 128), :])

    lane = lax.broadcasted_iota(jnp.int32, (128, 256), 1)

    def one_hot(low):
        return jnp.where(lane == jnp.concatenate([low, low], 1), 1.0, 0.0).astype(BF16)

    pl.semaphore_wait(barrier, GROUPS - 1 + SUBS - 1)

    def round_group(rows, send, recv):
        return [
            pltpu.make_async_remote_copy(
                src_ref=rows, dst_ref=rows, send_sem=send, recv_sem=recv,
                device_id=(g, lax.rem(s + i, SUBS)), device_id_type=MESH,
            )
            for i in range(1, SUBS)
        ]

    def drain(buffer, count, send, recv):
        part = buffer.at[pl.ds(0, count)]
        return pltpu.make_async_remote_copy(
            src_ref=part, dst_ref=part, send_sem=send, recv_sem=recv, device_id=(g, s), device_id_type=MESH
        )

    for copy in round_group(five.at[pl.ds(own, 128), :], five_send, five_recv):
        copy.start()

    slots[g] = pack[g]

    def send_and_build(i, carry):
        for q in range(SENDS):
            j = peer(SENDS * i + q)
            pltpu.make_async_remote_copy(
                src_ref=pack.at[j], dst_ref=slots.at[g], send_sem=slot_send, recv_sem=slot_recv,
                device_id=(j, s), device_id_type=MESH,
            ).start()
        for q in range(BUILD):
            c = BUILD * i + q
            hot5[pl.ds(pl.multiple_of(c * 128, 128), 128), :] = one_hot(column(low5[c // 128], c % 128))
        return carry

    lax.fori_loop(0, (GROUPS - 1) // SENDS, send_and_build, 0)
    for t in range(2):
        for h in range(2):
            hot3[pl.ds((2 * t + h) * 128, 128), :] = one_hot(jnp.bitwise_and(column(idx3[h], t), 255))
    picks3[...] = jnp.zeros((2048, K), F32)

    drain(five, 7 * 128, five_send, five_recv).wait_recv()
    four = ascend(five[...], 128, wide, up)
    lane4 = lax.broadcasted_iota(jnp.int32, (16, 128), 1)

    def lanes(c):
        return pl.ds(pl.multiple_of(c * K, K), K)

    def tiles(c, *parts):
        hot = hot5[pl.ds(pl.multiple_of(c * 128, 128), 128), :]
        block = column(idx5[c // 128], c % 128)
        for b, table, picks in parts:
            r = mm(hot, table)
            picked = jnp.where(block == 2 * b, r[:, :K], jnp.where(block == 2 * b + 1, r[:, K:], 0.0))
            picks[:, lanes(c)] = picked.astype(BF16)

    def near(i, carry, slots_too=False):
        first = jnp.concatenate([five[0:256, :], five[256:512, :]], 1)
        second = jnp.concatenate([five[512:768, :], five[768:1024, :]], 1)
        more = [(2, jnp.concatenate([store[0:256, :], store[256:512, :]], 1), picks2)] if slots_too else []
        base = i * STEP
        hot4 = []
        for q in range(STEP):
            c = base + q
            tiles(c, (0, first, picks0), (1, second, picks1), *more)
            hot4.append(jnp.where(lane4 == column(idx4[c // 128], c % 128), 1.0, 0.0))
        r4 = mm(jnp.concatenate(hot4, 0).astype(BF16), four)
        for q in range(STEP):
            picks43[0:16, lanes(base + q)] = r4[q * 16 : (q + 1) * 16].astype(BF16)
        return carry

    early = CLASSES // STEP - 1
    lax.fori_loop(0, early, near, 0)

    drain(slots, GROUPS - 1, slot_send, slot_recv).wait_recv()
    wide[0 : GROUPS * MESSAGE, :] = slots[...].astype(F32).reshape(GROUPS * MESSAGE, K)
    for k in range(CAP):
        store[k * GROUPS : (k + 1) * GROUPS, :] = wide[pl.ds(k, GROUPS, stride=MESSAGE), :].astype(BF16)
    store[GROUPS * CAP : 512, :] = jnp.zeros((512 - GROUPS * CAP, K), BF16)
    section = pl.multiple_of(s * SECT, SECT)
    for r in range(2):
        tops[pl.ds(pl.multiple_of(section + r * GROUPS, GROUPS), GROUPS), :] = wide[
            pl.ds(CAP + r, GROUPS, stride=MESSAGE), :
        ].astype(BF16)
    for copy in round_group(tops.at[pl.ds(section, SECT), :], rest_send, rest_recv):
        copy.start()

    lax.fori_loop(early, CLASSES // STEP, functools.partial(near, slots_too=True), 0)

    def far(i, carry):
        third = jnp.concatenate([store[0:256, :], store[256:512, :]], 1)
        for q in range(STEP):
            tiles(i * STEP + q, (2, third, picks2))
        return carry

    lax.fori_loop(0, early, far, 0)

    drain(tops, 7 * SECT, rest_send, rest_recv).wait_recv()
    quads = [
        mm(hot3[...], jnp.concatenate([tops[512 * b : 512 * b + 256, :], tops[512 * b + 256 : 512 * b + 512, :]], 1))
        for b in range(3)
    ]
    for t in range(2):
        for h in range(2):
            col = column(idx3[h], t)
            odd = jnp.bitwise_and(col, 256) != 0
            r = [x[(2 * t + h) * 128 : (2 * t + h + 1) * 128] for x in quads]
            r = [jnp.where(odd, x[:, 128:], x[:, :128]) for x in r]
            got = jnp.where(col >= 1024, r[2], jnp.where(col >= 512, r[1], r[0]))
            picks3[pl.ds(1024 * h + t, 128, stride=8), :] = jnp.where(col < 0, 0.0, got)

    loads[8].wait()

    def apply(i, total):
        base = i * STEP
        for q in range(STEP):
            c = base + q
            rows = picks3[pl.ds(pl.multiple_of(c * 8, 8), 8), :]
            picks43[16:32, lanes(c)] = jnp.concatenate([rows, rows], 0).astype(BF16)
        span = pl.ds(pl.multiple_of(base * K, K), STEP * K)
        picked = jnp.concatenate([picks0[:, span] + picks1[:, span] + picks2[:, span], picks43[:, span]], 0)
        return total + mm(picked, ops[pl.ds(base, STEP)].reshape(STEP * K, K))

    total = lax.fori_loop(0, CLASSES // STEP, apply, jnp.zeros((160, K), F32))

    loads[7].wait()
    local = total[144:152].astype(BF16)
    for c in range(8):
        wide[pl.ds(c, 8, stride=8), :] = mm(local, down[c])
    local = (wide[0:16, :] + total[128:144]).astype(BF16)
    for c in range(8):
        wide[pl.ds(c, 16, stride=8), :] = mm(local, down[c])
    local = (wide[0:128, :] + total[0:128]).astype(BF16)
    for c in range(8):
        out[pl.ds(c, 128, stride=8), :] = mm(local, down[c])

    drain(five, 7 * 128, five_send, five_recv).wait_send()
    drain(slots, GROUPS - 1, slot_send, slot_recv).wait_send()
    drain(tops, 7 * SECT, rest_send, rest_recv).wait_send()


def body(multipoles, up_ops, down_ops, far_ops, sources5, sources4, sources3, send_boxes, send_counts):
    dma = pltpu.SemaphoreType.DMA
    operands = (
        multipoles, up_ops, down_ops, sources5, sources4.T, sources3.T, send_boxes[0].T, send_counts, far_ops
    )
    return pl.pallas_call(
        kernel,
        out_shape=pltpu.VMEM((1024, K), F32),
        in_specs=[pl.BlockSpec(memory_space=pl.ANY)] * 9,
        out_specs=pl.BlockSpec(memory_space=pltpu.VMEM),
        scratch_shapes=[pltpu.VMEM(x.shape, x.dtype) for x in operands]
        + [
            pltpu.VMEM((NEAR, K), BF16),
            pltpu.VMEM((GROUPS * MESSAGE, K), F32),
            pltpu.VMEM((GROUPS, MESSAGE, K), BF16),
            pltpu.VMEM((GROUPS, MESSAGE, K), BF16),
            pltpu.VMEM((512, K), BF16),
            pltpu.VMEM((SUBS * SECT, K), BF16),
            pltpu.VMEM(((CLASSES + 1) * 128, 256), BF16),
            pltpu.VMEM((512, 256), BF16),
            pltpu.VMEM((128, CLASSES * K), BF16),
            pltpu.VMEM((128, CLASSES * K), BF16),
            pltpu.VMEM((128, CLASSES * K), BF16),
            pltpu.VMEM((32, CLASSES * K), BF16),
            pltpu.VMEM((2, 128, 128), jnp.int32),
            pltpu.VMEM((2, 128, 128), jnp.int32),
            pltpu.VMEM((2, 16, 128), jnp.int32),
            pltpu.VMEM((2, 128, 128), jnp.int32),
            pltpu.VMEM((256, 128), jnp.int32),
            pltpu.VMEM((1024, K), F32),
            pltpu.VMEM((2048, K), F32),
            dma((9,)),
        ]
        + [dma] * 6,
        compiler_params=pltpu.CompilerParams(
            collective_id=0, has_side_effects=True, vmem_limit_bytes=55 * 2**20
        ),
    )(*operands)


def solution(mesh):
    in_specs = (
        P(("grp", "sub"), None),
        P(),
        P(),
        P(),
        P(None, ("grp", "sub")),
        P(None, ("grp", "sub")),
        P(None, ("grp", "sub")),
        P(("grp", "sub"), None, None),
        P(("grp", "sub"), None),
    )
    out_specs = P(("grp", "sub"), None)
    return jax.shard_map(body, mesh=mesh, in_specs=in_specs, out_specs=out_specs, check_vma=False)
```
